32 devices in a mesh: horiz: 8 (over z, y), vert: 4 (over x, core).
Axes of the slice: x: 2, y: 2, z: 4, core: 2. Of those that a mesh axis runs over, the one named last changes fastest.
Arguments:
- tracer: bfloat16 [8, 2048, 128], P('vert', 'horiz'), may hold values from -6 to 6
- explicit_tiles: bfloat16 [8, 16, 7, 128, 128], P('vert', 'horiz'), may hold values from -0.25 to 0.25
- tile_columns: int32 [8, 16, 7], P('vert', 'horiz'), may hold values from 0 to 127, as said below
- tile_counts: int32 [8, 16], P('vert', 'horiz'), may hold values from 4 to 7
- surface_source: bfloat16 [2048, 128], P('horiz'), may hold values from -6 to 6
- implicit_columns: float32 [2048, 8, 8], P(('horiz', 'vert')), may hold values from -0.53033009 to 1
- settling: float32 [128], replicated, may hold values from 0.02 to 0.5
- wet_mask: int32 [8, 2048], P('vert', 'horiz'), may hold values 0 or 1
Outputs:
- tracer_out: bfloat16 [8, 2048, 128], P('vert', 'horiz')
The draws below stay inside these ranges and needn't reach their ends.
Inputs may be any that keep to these rules, and one draw needn't show every extreme that they name: `tile_columns`: slot 0 of block row (l, t) names the row's own tile l * 16 + t; the other slots name distinct tiles within 2 levels and 2 tiles of it, inside the grid.
All inputs are finite; a program needn't handle non-finite values. No bound on the sum of `wet_mask` on one device may be relied on, other than what follows from the above.
Results may differ from the reference program's by a relative error of at most 0.015.
Values may be sent and summed in bfloat16 or wider, within the bound.
A program may use at most 64 MiB of HBM per device.

```python
import math
import jax
import jax.numpy as jnp
from jax import lax

TILE = 128
CLASSES = 128
SLOTS = 7
REACH = 2
STEPS = 4
H_TILES = 16
H_CELLS = 2048
LEVELS = 8


def draw_tile_columns(key, part):
    side_width = 2 * REACH + 1
    candidate = jnp.arange(side_width * side_width, dtype=jnp.int32)
    level_step = candidate // side_width - REACH
    tile_step = candidate % side_width - REACH
    level_index = jnp.arange(LEVELS, dtype=jnp.int32)[:, None, None]
    tile_index = jnp.arange(H_TILES, dtype=jnp.int32)[None, :, None]
    full_shape = (LEVELS, H_TILES, side_width * side_width)
    near_level = jnp.broadcast_to(level_index + level_step[None, None, :], full_shape)
    near_tile = jnp.broadcast_to(tile_index + tile_step[None, None, :], full_shape)
    inside = (near_level >= 0) & (near_level < LEVELS) & (near_tile >= 0) & (near_tile < H_TILES)
    centre = (level_step == 0) & (tile_step == 0)
    random_bits = jax.random.randint(key, full_shape, 0, 1 << 20)
    scores = random_bits * 64 + candidate[None, None, :]
    scores = jnp.where(inside, scores, -1 - candidate[None, None, :])
    scores = jnp.where(centre[None, None, :], 1 << 28, scores)
    unused, chosen = lax.top_k(scores, SLOTS)
    pick_level = jnp.take_along_axis(near_level, chosen, axis=2)
    pick_tile = jnp.take_along_axis(near_tile, chosen, axis=2)
    return (pick_level * H_TILES + pick_tile).astype(jnp.int32)


def draw_implicit_columns(key, part):
    key_diag = jax.random.fold_in(key, 11)
    key_off = jax.random.fold_in(key, 23)
    identity = jnp.eye(LEVELS, dtype=jnp.float32)
    diagonal = jax.random.uniform(key_diag, (H_CELLS, LEVELS, 1), jnp.float32, 0.6, 1.0)
    limit = 1.5 / LEVELS ** 0.5
    spread = jax.random.normal(key_off, (H_CELLS, LEVELS, LEVELS), jnp.float32) * (0.3 / LEVELS ** 0.5)
    spread = jnp.clip(spread, -limit, limit)
    return identity * diagonal + (1.0 - identity) * spread


def set_ends(array, rng, least, high):
    longest = array.shape.index(max(array.shape))
    spots = []
    for shift in (0, 1):
        where = [jax.random.randint(jax.random.fold_in(rng, axis), (), 0, length) for axis, length in enumerate(array.shape)]
        where[longest] = (where[longest] + shift) % array.shape[longest]
        spots.append(tuple(where))
    return array.at[spots[0]].set(least).at[spots[1]].set(high)


def shard_levels(stream_key, extent, shards, low, high):
    def one(dim, parts):
        heights = jax.random.uniform(jax.random.fold_in(jax.random.fold_in(stream_key, 6), dim), (parts,), jnp.float32, low / len(shards), high / len(shards))
        return jnp.repeat(jnp.exp(heights), extent[dim] // parts).reshape((-1,) + (1,) * (len(extent) - dim - 1))

    loudness = one(*shards[0])
    for cut in shards[1:]:
        loudness = loudness * one(*cut)
    return loudness


def gaussian(own_key, shape, deviation, most, split=(), kind=jnp.bfloat16):
    factor_of = shard_levels(own_key, shape, split, -0.22, 0.18) if split else 1.0
    entries = jax.random.normal(own_key, shape, jnp.float32) * deviation * factor_of
    return jnp.minimum(jnp.maximum(entries, -most), most).astype(kind)


def setup_inputs(seed: int = 0) -> dict:
    key_list = jax.random.split(jax.random.key(seed), 9)
    tracer = gaussian(key_list[0], (LEVELS, H_CELLS, CLASSES), 1.0, 6.0, ((0, 4), (1, 8)))
    explicit_tiles = gaussian(key_list[1], (LEVELS, H_TILES, SLOTS, TILE, TILE), (TILE * 5) ** -0.5, 0.25, ((0, 4), (1, 8)))
    tile_columns = draw_tile_columns(jax.random.fold_in(key_list[8], 71), 0)
    tile_counts = set_ends(jax.random.randint(key_list[3], (LEVELS, H_TILES), 4, 8), jax.random.fold_in(key_list[3], 1), 4, 7).astype(jnp.int32)
    surface_source = gaussian(key_list[4], (H_CELLS, CLASSES), 1.0, 6.0, ((0, 8),))
    implicit_columns = draw_implicit_columns(jax.random.fold_in(key_list[8], 71), 0)
    settling = jnp.clip(jnp.exp(jax.random.uniform(key_list[6], (CLASSES,), jnp.float32, math.log(0.02), math.log(0.5))), 0.02, 0.5)
    wet_mask = set_ends((jax.random.randint(key_list[7], (LEVELS, H_CELLS), 0, 8) < 7).astype(jnp.int32), jax.random.fold_in(key_list[7], 1), 0, 1)
    return dict(tracer=tracer, explicit_tiles=explicit_tiles, tile_columns=tile_columns, tile_counts=tile_counts, surface_source=surface_source, implicit_columns=implicit_columns, settling=settling, wet_mask=wet_mask)


def reference(tracer, explicit_tiles, tile_columns, tile_counts, surface_source, implicit_columns, settling, wet_mask):
    levels, cell_count, classes = tracer.shape
    tile_size = explicit_tiles.shape[-1]
    h_tiles = cell_count // tile_size
    slot_count = explicit_tiles.shape[2]
    live_slots = (jnp.arange(slot_count, dtype=jnp.int32)[None, None, :] < tile_counts[:, :, None]).astype(jnp.float32)
    fall_rate = settling[None, None, :]
    wet_cells = wet_mask.astype(jnp.float32)[:, :, None]
    current = tracer
    for step_index in range(STEPS):
        all_blocks = current.reshape(levels * h_tiles, tile_size, classes)

        def level_rows(inputs):
            tiles_here, columns_here, live_here = inputs
            picked = all_blocks[columns_here].astype(jnp.float32) * live_here[:, :, None, None]
            return jnp.einsum("tjab,tjbs->tas", tiles_here.astype(jnp.float32), picked)

        explicit_flow = lax.map(level_rows, (explicit_tiles, tile_columns, live_slots))
        explicit_flow = explicit_flow.reshape(levels, cell_count, classes)
        explicit_flow = explicit_flow.at[0].add(surface_source.astype(jnp.float32))
        loaded = explicit_flow.astype(jnp.bfloat16)
        mixed_col = jnp.einsum("ckm,mcs->kcs", implicit_columns, loaded.astype(jnp.float32), precision=lax.Precision.HIGHEST)
        from_above = jnp.concatenate([jnp.zeros_like(mixed_col[:1]), mixed_col[:-1]], axis=0)
        settled = (1.0 - fall_rate) * mixed_col + fall_rate * from_above
        current = (wet_cells * settled).astype(jnp.bfloat16)
    return current
```

```python
import functools

import jax
import jax.numpy as jnp
from jax import lax
from jax.experimental import pallas as pl
from jax.experimental.pallas import tpu as pltpu
from jax.sharding import PartitionSpec as P

REACH = 2
STEPS = 4
Q = 2
MESH = pl.DeviceIdType.MESH
F32 = jnp.float32
BF16 = jnp.bfloat16


def kernel(
    h_size,
    v_size,
    tracer,
    tiles,
    source,
    extra,
    settling,
    columns,
    counts,
    out,
    weights,
    gath,
    other,
    src_t,
    fall,
    ops,
    a_win,
    w_win,
    pos,
    send_sem,
    recv_sem,
    ops_send,
    ops_recv,
    *halos,
):
    lev_dev, cells_dev, classes = tracer.shape
    slots, size = tiles.shape[2], tiles.shape[3]
    tiles_dev = cells_dev // size
    window = lev_dev + 2 * REACH
    levels = lev_dev * v_size
    h_tiles = h_size * tiles_dev
    ch = classes // Q
    h = lax.axis_index("horiz")
    v = lax.axis_index("vert")
    even = lax.rem(h, 2) == 0
    core = lax.rem(v, 2)
    base = 2 * (v // 2)
    partner = jnp.where(even, h + 1, h - 1)
    ahead = jnp.where(even, h + 2, h - 2)
    behind = jnp.where(even, h - 2, h + 2)
    has_ahead = (ahead >= 0) & (ahead < h_size)
    has_behind = (behind >= 0) & (behind < h_size)

    def vert(d):
        flipped = v
        if d & 1:
            flipped = flipped + 1 - 2 * core
        if d & 2:
            flipped = lax.rem(flipped + 2, 4)
        return {"horiz": h, "vert": flipped}

    near = {"horiz": partner, "vert": v}
    front = {"horiz": ahead, "vert": v}
    back = {"horiz": behind, "vert": v}

    barrier = pltpu.get_barrier_semaphore()
    for d in (1, 2, 3):
        pl.semaphore_signal(barrier, inc=1, device_id=vert(d), device_id_type=MESH)
    pl.semaphore_signal(barrier, inc=1, device_id=near, device_id_type=MESH)

    @pl.when(has_ahead)
    def _():
        pl.semaphore_signal(barrier, inc=1, device_id=front, device_id_type=MESH)

    @pl.when(has_behind)
    def _():
        pl.semaphore_signal(barrier, inc=1, device_id=back, device_id_type=MESH)

    own_t = 2 + core
    near_t = jnp.where(even, 4, 0) + core
    far_t = jnp.where(even, 0, 4) + core

    def remote(src, dst, p, q, kind, where):
        return pltpu.make_async_remote_copy(
            src_ref=src,
            dst_ref=dst,
            send_sem=send_sem.at[p, q, kind],
            recv_sem=recv_sem.at[p, q, kind],
            device_id=where,
            device_id_type=MESH,
        )

    def x_copies(p, q):
        par = p % 2
        here = gath.at[par, q, pl.ds(lev_dev * v, lev_dev)]
        return [
            remote(here if d == 2 else other.at[par, q], here, p, q, d - 1, vert(d))
            for d in (2, 3, 1)
        ]

    def block(p, q, where):
        return halos[p % 2 * Q + q].at[pl.ds(where * window, window)]

    def near_copy(p, q):
        return remote(block(p, q, own_t), block(p, q, far_t), p, q, 3, near)

    def side_own(p, q):
        return remote(block(p, q, own_t), block(p, q, own_t), p, q, 4, vert(1))

    def front_copy(p, q):
        return remote(block(p, q, near_t), block(p, q, far_t), p, q, 5, front)

    def side_near(p, q):
        return remote(block(p, q, near_t), block(p, q, near_t), p, q, 6, vert(1))

    def side_far(p, q):
        return remote(block(p, q, far_t), block(p, q, far_t), p, q, 7, vert(1))

    def put(p, q, on_core, level, value):
        if on_core:
            gath[p % 2, q, lev_dev * v + level] = value
        else:
            other[p % 2, q, level] = value

    def load_first(q):
        for on_core in (False, True):
            t = core if on_core else 1 - core
            for level in range(lev_dev):
                tile = tracer[level, pl.ds(pl.multiple_of(t * size, size), size), :]
                value = tile.T[q * ch : (q + 1) * ch]
                put(0, q, on_core, level, value)

    def explicit(p, q):
        for on_core in (False, True):
            t = core if on_core else 1 - core
            for level in range(lev_dev):
                picked = jnp.concatenate(
                    [
                        halos[(p - 1) % 2 * Q + q][pos[level, t * slots + j]]
                        for j in range(slots)
                    ],
                    axis=1,
                )
                flow = jnp.dot(
                    picked, weights[level, t], preferred_element_type=F32
                )
                if level == 0:
                    flow = flow + src_t[t, q * ch : (q + 1) * ch, :]
                put(p, q, on_core, level, flow.astype(BF16))

    def stage_a(p, q):
        if p == 0:
            load_first(q)
        else:
            explicit(p, q)
        if p == 0 and q == 0:
            count = 4 + has_ahead.astype(jnp.int32) + has_behind.astype(jnp.int32)
            pl.semaphore_wait(barrier, count)
        for copy in x_copies(p, q):
            copy.start()

    def sends_done(p, q):
        for copy in x_copies(p, q):
            copy.wait_send()
        side_own(p, q).wait_send()
        if p == STEPS:
            return
        near_copy(p, q).wait_send()
        side_near(p, q).wait_send()

        @pl.when(has_ahead)
        def _():
            front_copy(p, q).wait_send()

        @pl.when(has_behind)
        def _():
            side_far(p, q).wait_send()

    def solve(p, q):
        par = p % 2
        halo = halos[par * Q + q]
        first = own_t * window
        if p == 0:
            for k in range(window):
                halo[first + k] = gath[par, q, base + k]
            return
        rows = 16

        def body(i, carry):
            at = pl.ds(pl.multiple_of(i * rows, rows), rows)
            loaded = [gath[par, q, m, at, :].astype(F32) for m in range(levels)]
            rate = fall[pl.ds(pl.multiple_of(q * ch + i * rows, rows), rows), :]
            stay = 1.0 - rate
            above = None
            for k in range(window + 1):
                a = a_win[k * levels : (k + 1) * levels, :]
                mixed = a[0:1] * loaded[0]
                for m in range(1, levels):
                    mixed = mixed + a[m : m + 1] * loaded[m]
                if k:
                    settled = stay * mixed + rate * above
                    wet = w_win[k - 1 : k, :]
                    halo[first + k - 1, at, :] = (wet * settled).astype(BF16)
                above = mixed
            return carry

        lax.fori_loop(0, ch // rows, body, 0)

    def stage_b(p, q):
        for copy in x_copies(p, q):
            copy.wait_recv()
        if p:
            sends_done(p - 1, q)
        solve(p, q)
        if p < STEPS:
            near_copy(p, q).start()
        side_own(p, q).start()

    def stage_c(p, q):
        near_copy(p, q).wait_recv()

        @pl.when(has_ahead)
        def _():
            front_copy(p, q).start()

        side_near(p, q).start()

    def stage_d(p, q):
        @pl.when(has_behind)
        def _():
            front_copy(p, q).wait_recv()
            side_far(p, q).start()

    def stage_e(p, q):
        side_own(p, q).wait_recv()
        side_near(p, q).wait_recv()

        @pl.when(has_behind)
        def _():
            side_far(p, q).wait_recv()

    def ops_copy(d):
        return pltpu.make_async_remote_copy(
            src_ref=extra,
            dst_ref=ops.at[v],
            send_sem=ops_send.at[d - 1],
            recv_sem=ops_recv.at[d - 1],
            device_id=vert(d),
            device_id_type=MESH,
        )

    def prepare():
        for level in range(lev_dev):
            for t in range(tiles_dev):
                for j in range(slots):
                    column = columns[level, t * slots + j]
                    row = lax.div(column, h_tiles) - base
                    across = lax.rem(column, h_tiles) - tiles_dev * h + REACH
                    last = 3 * tiles_dev * window - 1
                    pos[level, t * slots + j] = jnp.clip(across * window + row, 0, last)
                    live = (j < counts[level, t]).astype(F32)
                    weights[level, t, j * size : (j + 1) * size, :] = (
                        tiles[level, t, j].astype(F32).T * live
                    ).astype(BF16)
        on_top = (v == 0).astype(F32)
        for t in range(tiles_dev):
            src_t[t] = source[t * size : (t + 1) * size, :].astype(F32).T * on_top
        fall[...] = jnp.broadcast_to(settling[...], (size, classes)).T

    ops[v] = extra[...]
    for q in range(Q):
        stage_a(0, q)
    for d in (1, 2, 3):
        ops_copy(d).start()
    prepare()
    for q in range(Q):
        stage_b(0, q)
    for d in (1, 2, 3):
        ops_copy(d).wait()
    square = levels * levels
    for k in range(window + 1):
        level = base + k - 1
        row = pl.ds(pl.multiple_of(jnp.maximum(level, 0) * levels, levels), levels)
        keep = (level >= 0).astype(F32)
        a_win[k * levels : (k + 1) * levels, :] = keep * (
            ops[2 * core, row, :] + ops[2 * core + 1, row, :]
        )
        if k:
            w_win[k - 1 : k, :] = ops[
                level // lev_dev,
                pl.ds(square + lax.rem(level, lev_dev) * tiles_dev + core, 1),
                :,
            ]
    for p in range(STEPS):
        for q in range(Q):
            stage_c(p, q)
        for q in range(Q):
            stage_d(p, q)
        for q in range(Q):
            stage_e(p, q)
            stage_a(p + 1, q)
        for q in range(Q):
            stage_b(p + 1, q)
    for q in range(Q):
        side_own(STEPS, q).wait_recv()
    for level in range(lev_dev):
        for t in range(tiles_dev):
            where = (2 + t) * window + lev_dev * v - base + level
            whole = jnp.concatenate(
                [halos[STEPS % 2 * Q + q][where] for q in range(Q)], axis=0
            )
            out[level, t * size : (t + 1) * size, :] = whole.T
    for q in range(Q):
        sends_done(STEPS, q)


def on_device(h_size, v_size, tracer, tiles, columns, counts, source, implicit, settling, wet):
    lev_dev, cells_dev, classes = tracer.shape
    slots, size = tiles.shape[2], tiles.shape[3]
    tiles_dev = cells_dev // size
    levels = implicit.shape[1]
    share = implicit.shape[0]
    window = lev_dev + 2 * REACH
    assert lev_dev == 2 and tiles_dev == 2 and v_size == 4 and h_size % 2 == 0
    ch = classes // Q
    flat = implicit.reshape(share, levels * levels).T
    right = lax.rem(lax.axis_index("vert"), 2).astype(F32)
    flat = jnp.concatenate([flat * (1.0 - right), flat * right], axis=1)
    wet_rows = wet.astype(F32).reshape(lev_dev * tiles_dev, size)
    extra = jnp.concatenate([flat, wet_rows, jnp.zeros_like(wet_rows)], axis=0)
    vm = pl.BlockSpec(memory_space=pltpu.VMEM)
    sm = pl.BlockSpec(memory_space=pltpu.SMEM)
    phases = STEPS + 1
    return pl.pallas_call(
        functools.partial(kernel, h_size, v_size),
        out_shape=jax.ShapeDtypeStruct(tracer.shape, tracer.dtype),
        in_specs=[vm] * 5 + [sm] * 2,
        out_specs=vm,
        scratch_shapes=[
            pltpu.VMEM((lev_dev, tiles_dev, slots * size, size), BF16),
            pltpu.VMEM((2, Q, levels, ch, size), BF16),
            pltpu.VMEM((2, Q, lev_dev, ch, size), BF16),
            pltpu.VMEM((tiles_dev, classes, size), F32),
            pltpu.VMEM((classes, size), F32),
            pltpu.VMEM((v_size,) + extra.shape, F32),
            pltpu.VMEM(((window + 1) * levels, size), F32),
            pltpu.VMEM((8, size), F32),
            pltpu.SMEM((lev_dev, tiles_dev * slots), jnp.int32),
            pltpu.SemaphoreType.DMA((phases, Q, 8)),
            pltpu.SemaphoreType.DMA((phases, Q, 8)),
            pltpu.SemaphoreType.DMA((3,)),
            pltpu.SemaphoreType.DMA((3,)),
        ]
        + [pltpu.VMEM((3 * tiles_dev * window, ch, size), BF16)] * (2 * Q),
        compiler_params=pltpu.CompilerParams(
            collective_id=0, has_side_effects=True, vmem_limit_bytes=32 * 2**20
        ),
    )(
        tracer,
        tiles,
        source,
        extra,
        settling.reshape(1, classes),
        columns.reshape(lev_dev, tiles_dev * slots),
        counts,
    )


def solution(mesh):
    placed = (
        P("vert", "horiz", None),
        P("vert", "horiz", None, None, None),
        P("vert", "horiz", None),
        P("vert", "horiz"),
        P("horiz", None),
        P(("horiz", "vert"), None, None),
        P(),
        P("vert", "horiz"),
    )
    body = functools.partial(on_device, mesh.shape["horiz"], mesh.shape["vert"])
    return jax.shard_map(
        body, mesh=mesh, in_specs=placed, out_specs=P("vert", "horiz", None), check_vma=False
    )
```

```python
import functools

import jax
import jax.numpy as jnp
from jax import lax
from jax.experimental import pallas as pl
from jax.experimental.pallas import tpu as pltpu
from jax.sharding import PartitionSpec as P

REACH = 2
STEPS = 4
Q = 4
MESH = pl.DeviceIdType.MESH
F32 = jnp.float32
BF16 = jnp.bfloat16


def kernel(
    h_size,
    v_size,
    tracer,
    tiles,
    source,
    extra,
    settling,
    columns,
    counts,
    out,
    weights,
    turned,
    gath,
    other,
    final,
    src_t,
    fall,
    ops,
    a_win,
    w_win,
    cols_v,
    cols_s,
    pos,
    send_sem,
    recv_sem,
    first_send,
    first_recv,
    last_send,
    last_recv,
    ops_send,
    ops_recv,
    pair_send,
    pair_recv,
    local_sem,
    *halos,
):
    lev_dev, cells_dev, classes = tracer.shape
    slots, size = tiles.shape[2], tiles.shape[3]
    tiles_dev = cells_dev // size
    window = lev_dev + 2 * REACH
    levels = lev_dev * v_size
    lev_chip = 2 * lev_dev
    h_tiles = h_size * tiles_dev
    half = classes // 2
    ch = half // Q
    blk = tiles_dev * window
    h = lax.axis_index("horiz")
    v = lax.axis_index("vert")
    even = lax.rem(h, 2) == 0
    core = lax.rem(v, 2)
    chip = v // 2
    base = 2 * chip
    partner = jnp.where(even, h + 1, h - 1)
    ahead = jnp.where(even, h + 2, h - 2)
    behind = jnp.where(even, h - 2, h + 2)
    has_ahead = (ahead >= 0) & (ahead < h_size)
    has_behind = (behind >= 0) & (behind < h_size)

    def vert(d):
        flipped = v
        if d & 1:
            flipped = flipped + 1 - 2 * core
        if d & 2:
            flipped = lax.rem(flipped + 2, 4)
        return {"horiz": h, "vert": flipped}

    near = {"horiz": partner, "vert": v}
    front = {"horiz": ahead, "vert": v}
    back = {"horiz": behind, "vert": v}

    barrier = pltpu.get_barrier_semaphore()
    for where in (vert(1), vert(2), vert(3), near):
        pl.semaphore_signal(barrier, inc=1, device_id=where, device_id_type=MESH)

    @pl.when(has_ahead)
    def _():
        pl.semaphore_signal(barrier, inc=1, device_id=front, device_id_type=MESH)

    @pl.when(has_behind)
    def _():
        pl.semaphore_signal(barrier, inc=1, device_id=back, device_id_type=MESH)

    near_at = jnp.where(even, 2 * blk, 0)
    far_at = jnp.where(even, 0, 2 * blk)

    def copy_to(src, dst, send, recv, where):
        return pltpu.make_async_remote_copy(
            src_ref=src,
            dst_ref=dst,
            send_sem=send,
            recv_sem=recv,
            device_id=where,
            device_id_type=MESH,
        )

    def remote(src, dst, p, q, kind, where):
        return copy_to(
            src, dst, send_sem.at[p, q, kind], recv_sem.at[p, q, kind], where
        )

    def x_copies(p, q):
        if p == 0:
            here = gath.at[0, q, pl.ds(lev_dev * v, lev_dev)]
            return [
                copy_to(
                    here if d == 2 else other.at[q],
                    here,
                    first_send.at[q, d - 1],
                    first_recv.at[q, d - 1],
                    vert(d),
                )
                for d in (2, 3, 1)
            ]
        here = gath.at[p % 2, q, pl.ds(lev_chip * chip, lev_chip)]
        return [remote(here, here, p, q, 0, vert(2))]

    def block(p, q, at):
        return halos[p % 2 * Q + q].at[pl.ds(at, blk)]

    def near_copy(p, q):
        return remote(block(p, q, blk), block(p, q, far_at), p, q, 1, near)

    def front_copy(p, q):
        return remote(block(p, q, near_at), block(p, q, far_at), p, q, 2, front)

    def last_copies(q):
        theirs = lev_dev * (v + 1 - 2 * core) - base
        halo = halos[STEPS % 2 * Q + q]
        return [
            copy_to(
                halo.at[pl.ds(blk + t * window + theirs, lev_dev)],
                final.at[core * Q + q, t],
                last_send.at[q, t],
                last_recv.at[q, t],
                vert(1),
            )
            for t in range(tiles_dev)
        ]

    def pair_copies():
        mine = weights.at[pl.ds(lev_dev * core, lev_dev)]
        cols = cols_v.at[core]
        return [
            copy_to(cols, cols, pair_send.at[0], pair_recv.at[0], vert(1)),
            copy_to(mine, mine, pair_send.at[1], pair_recv.at[1], vert(1)),
        ]

    def load_first(q):
        for level in range(lev_dev):
            for t in range(tiles_dev):
                ours = pl.ds(pl.multiple_of(core * half + q * ch, ch), ch)
                theirs = pl.ds(pl.multiple_of((1 - core) * half + q * ch, ch), ch)
                gath[0, q, lev_dev * v + level, t] = turned[level, t, ours, :]
                other[q, level, t] = turned[level, t, theirs, :]

    def explicit(p, q):
        for level in range(lev_chip):
            for t in range(tiles_dev):
                picked = jnp.concatenate(
                    [
                        halos[(p - 1) % 2 * Q + q][pos[level, t * slots + j]]
                        for j in range(slots)
                    ],
                    axis=1,
                )
                flow = jnp.dot(
                    picked, weights[level, t], preferred_element_type=F32
                )
                if level == 0:
                    ours = pl.ds(pl.multiple_of(core * half + q * ch, ch), ch)
                    flow = flow + src_t[t, ours, :]
                gath[p % 2, q, lev_chip * chip + level, t] = flow.astype(BF16)

    def stage_a(p, q):
        if p == 0:
            load_first(q)
        else:
            explicit(p, q)
        for copy in x_copies(p, q):
            copy.start()

    def sends_done(p, q):
        for copy in x_copies(p, q):
            copy.wait_send()
        if p == STEPS:
            return
        near_copy(p, q).wait_send()

        @pl.when(has_ahead)
        def _():
            front_copy(p, q).wait_send()

    def solve(p, q):
        par = p % 2
        halo = halos[par * Q + q]
        if p == 0:
            for t in range(tiles_dev):
                for k in range(window):
                    halo[blk + t * window + k] = gath[par, q, base + k, t]
            return
        rows = 16

        for t in range(tiles_dev):
            for i in range(ch // rows):
                at = slice(i * rows, (i + 1) * rows)
                loaded = [gath[par, q, m, t, at, :].astype(F32) for m in range(levels)]
                start = core * half + q * ch + i * rows
                rate = fall[pl.ds(pl.multiple_of(start, rows), rows), :]
                stay = 1.0 - rate
                above = None
                for k in range(window + 1):
                    mixed = None
                    for m in range(levels):
                        r = k * levels + m
                        term = a_win[t, r : r + 1, :] * loaded[m]
                        mixed = term if m == 0 else mixed + term
                    if k:
                        settled = stay * mixed + rate * above
                        wet = w_win[t, k - 1 : k, :]
                        halo[blk + t * window + k - 1, at, :] = (wet * settled).astype(BF16)
                    above = mixed

    def stage_b(p, q):
        for copy in x_copies(p, q):
            copy.wait_recv()
        if p:
            sends_done(p - 1, q)
        solve(p, q)
        if p < STEPS:
            near_copy(p, q).start()
        else:
            for copy in last_copies(q):
                copy.start()

    def stage_c(p, q):
        near_copy(p, q).wait_recv()

        @pl.when(has_ahead)
        def _():
            front_copy(p, q).start()

    def stage_d(p, q):
        @pl.when(has_behind)
        def _():
            front_copy(p, q).wait_recv()

    def ops_copy(d):
        return copy_to(
            extra, ops.at[v], ops_send.at[d - 1], ops_recv.at[d - 1], vert(d)
        )

    def prepare():
        for level in range(lev_dev):
            for t in range(tiles_dev):
                for j in range(slots):
                    live = (j < counts[level, t]).astype(F32)
                    weights[lev_dev * core + level, t, j * size : (j + 1) * size, :] = (
                        tiles[level, t, j].astype(F32).T * live
                    ).astype(BF16)

    def prepare_more():
        on_top = (chip == 0).astype(F32)
        for t in range(tiles_dev):
            src_t[t] = source[t * size : (t + 1) * size, :].astype(F32).T * on_top
        fall[...] = jnp.broadcast_to(settling[...], (size, classes)).T

    def positions():
        local = pltpu.make_async_copy(cols_v, cols_s, local_sem)
        local.start()
        local.wait()
        last = 3 * blk - 1
        for level in range(lev_chip):
            for n in range(tiles_dev * slots):
                column = cols_s[level // lev_dev, level % lev_dev, n]
                row = lax.div(column, h_tiles) - base
                across = lax.rem(column, h_tiles) - tiles_dev * h + REACH
                pos[level, n] = jnp.clip(across * window + row, 0, last)

    def operators():
        square = levels * levels
        for t in range(tiles_dev):
            for k in range(window + 1):
                level = base + k - 1
                row = pl.ds(
                    pl.multiple_of(jnp.maximum(level, 0) * levels, levels), levels
                )
                keep = (level >= 0).astype(F32)
                a_win[t, k * levels : (k + 1) * levels, :] = keep * (
                    ops[2 * t, row, :] + ops[2 * t + 1, row, :]
                )
                if k:
                    w_win[t, k - 1 : k, :] = ops[
                        level // lev_dev,
                        pl.ds(square + lax.rem(level, lev_dev) * tiles_dev + t, 1),
                        :,
                    ]

    ops[v] = extra[...]
    cols_v[core] = columns[...]
    for level in range(lev_dev):
        for t in range(tiles_dev):
            turned[level, t] = tracer[level, t * size : (t + 1) * size, :].T
    count = 4 + has_ahead.astype(jnp.int32) + has_behind.astype(jnp.int32)
    pl.semaphore_wait(barrier, count)
    for q in range(Q):
        stage_a(0, q)
    for d in (1, 2, 3):
        ops_copy(d).start()
    pair = pair_copies()
    pair[0].start()
    prepare()
    pair[1].start()
    for q in range(Q):
        stage_b(0, q)
    prepare_more()
    for d in (1, 2, 3):
        ops_copy(d).wait()
    operators()
    pair[0].wait()
    positions()
    for p in range(STEPS):
        for q in range(Q):
            stage_c(p, q)
        if p == 0:
            pair[1].wait()
        for q in range(Q):
            stage_d(p, q)
            stage_a(p + 1, q)
        for q in range(Q):
            stage_b(p + 1, q)
    mine = lev_dev * v - base
    for q in range(Q):
        for t in range(tiles_dev):
            for level in range(lev_dev):
                final[core * Q + q, t, level] = halos[STEPS % 2 * Q + q][
                    blk + t * window + mine + level
                ]
    for q in range(Q):
        for copy in last_copies(q):
            copy.wait_recv()
    for level in range(lev_dev):
        for t in range(tiles_dev):
            whole = jnp.concatenate(
                [final[i, t, level] for i in range(2 * Q)], axis=0
            )
            out[level, t * size : (t + 1) * size, :] = whole.T
    for q in range(Q):
        sends_done(STEPS, q)
        for copy in last_copies(q):
            copy.wait_send()


def on_device(h_size, v_size, tracer, tiles, columns, counts, source, implicit, settling, wet):
    lev_dev, cells_dev, classes = tracer.shape
    slots, size = tiles.shape[2], tiles.shape[3]
    tiles_dev = cells_dev // size
    levels = implicit.shape[1]
    share = implicit.shape[0]
    window = lev_dev + 2 * REACH
    assert lev_dev == 2 and tiles_dev == 2 and v_size == 4 and h_size % 2 == 0
    ch = classes // 2 // Q
    flat = implicit.reshape(share, levels * levels).T
    right = lax.rem(lax.axis_index("vert"), 2).astype(F32)
    flat = jnp.concatenate([flat * (1.0 - right), flat * right], axis=1)
    wet_rows = wet.astype(F32).reshape(lev_dev * tiles_dev, size)
    extra = jnp.concatenate([flat, wet_rows, jnp.zeros_like(wet_rows)], axis=0)
    vm = pl.BlockSpec(memory_space=pltpu.VMEM)
    sm = pl.BlockSpec(memory_space=pltpu.SMEM)
    phases = STEPS + 1
    cols = columns.reshape(lev_dev, tiles_dev * slots)
    cols = jnp.pad(cols, ((0, 8 - lev_dev), (0, 128 - cols.shape[1])))
    dma = pltpu.SemaphoreType.DMA
    return pl.pallas_call(
        functools.partial(kernel, h_size, v_size),
        out_shape=jax.ShapeDtypeStruct(tracer.shape, tracer.dtype),
        in_specs=[vm] * 6 + [sm],
        out_specs=vm,
        scratch_shapes=[
            pltpu.VMEM((2 * lev_dev, tiles_dev, slots * size, size), BF16),
            pltpu.VMEM((lev_dev, tiles_dev, classes, size), BF16),
            pltpu.VMEM((2, Q, levels, tiles_dev, ch, size), BF16),
            pltpu.VMEM((Q, lev_dev, tiles_dev, ch, size), BF16),
            pltpu.VMEM((2 * Q, tiles_dev, lev_dev, ch, size), BF16),
            pltpu.VMEM((tiles_dev, classes, size), F32),
            pltpu.VMEM((classes, size), F32),
            pltpu.VMEM((v_size,) + extra.shape, F32),
            pltpu.VMEM((tiles_dev, (window + 1) * levels, size), F32),
            pltpu.VMEM((tiles_dev, 8, size), F32),
            pltpu.VMEM((2,) + cols.shape, jnp.int32),
            pltpu.SMEM((2,) + cols.shape, jnp.int32),
            pltpu.SMEM((2 * lev_dev, tiles_dev * slots), jnp.int32),
            dma((phases, Q, 3)),
            dma((phases, Q, 3)),
            dma((Q, 3)),
            dma((Q, 3)),
            dma((Q, tiles_dev)),
            dma((Q, tiles_dev)),
            dma((3,)),
            dma((3,)),
            dma((2,)),
            dma((2,)),
            dma(()),
        ]
        + [pltpu.VMEM((3 * tiles_dev * window, ch, size), BF16)] * (2 * Q),
        compiler_params=pltpu.CompilerParams(
            collective_id=0, has_side_effects=True, vmem_limit_bytes=32 * 2**20
        ),
    )(tracer, tiles, source, extra, settling.reshape(1, classes), cols, counts)


def solution(mesh):
    placed = (
        P("vert", "horiz", None),
        P("vert", "horiz", None, None, None),
        P("vert", "horiz", None),
        P("vert", "horiz"),
        P("horiz", None),
        P(("horiz", "vert"), None, None),
        P(),
        P("vert", "horiz"),
    )
    body = functools.partial(on_device, mesh.shape["horiz"], mesh.shape["vert"])
    return jax.shard_map(
        body, mesh=mesh, in_specs=placed, out_specs=P("vert", "horiz", None), check_vma=False
    )
```
